512 devices in a mesh: blk: 128 (over x, y_lo, z), head: 4 (over y_hi, core).
Axes of the slice: x: 4, y: 8 (y_hi: 2, y_lo: 4; y = y_hi * 4 + y_lo), z: 8, core: 2. Of those that a mesh axis runs over, the one named last changes fastest.
Arguments:
- queries: bfloat16 [65536, 2048], P(('blk', 'head')), may hold values from -32 to 32
- keys: bfloat16 [65536, 512], P(('blk', 'head')), may hold values from -32 to 32
- values: bfloat16 [65536, 512], P(('blk', 'head')), may hold values from -6 to 6
- frame_of: int32 [512], replicated, may hold values from 0 to 511, each once
- counts: int32 [512], replicated, may hold values from 64 to 128
Outputs:
- attended: bfloat16 [65536, 2048], P(('blk', 'head'))
The draws below stay inside these ranges and needn't reach their ends.
Inputs may be any that keep to these rules, and one draw needn't show every extreme that they name: `frame_of`: every value from 0 to 511 appears once.
All inputs are finite; a program needn't handle non-finite values.
Results may differ from the reference program's by a relative error of at most 0.006.
Values may be sent and summed in bfloat16 or wider, within the bound.
No kernel may reach another device: no remote copies, remote signals or barrier semaphores. Data moves between devices by JAX's collectives and lax.ppermute only.
A program may use at most 64 MiB of HBM per device.

```python
import jax
import jax.numpy as jnp
from jax import lax

HEAD_DIM = 128
Q_HEADS = 16
KV_HEADS = 4
FRAME_TOK = 128
FRAME_DEV = 1
CYCLE = 4
FRAMES = 512
SLOTS = 65536
N_BLK = 128
N_HEAD = 4


def draw_queries(key, part):
    key = jax.random.fold_in(key, 1)
    row_width = Q_HEADS * HEAD_DIM
    drawn = jnp.clip(jax.random.normal(key, (SLOTS, row_width), jnp.float32), -6.0, 6.0)
    return drawn.astype(jnp.bfloat16)


def draw_keys(key, part):
    key = jax.random.fold_in(key, 2)
    row_width = KV_HEADS * HEAD_DIM
    drawn = jnp.clip(jax.random.normal(key, (SLOTS, row_width), jnp.float32), -6.0, 6.0)
    return drawn.astype(jnp.bfloat16)


def set_ends(values, rng, low, high):
    longest = values.shape.index(max(values.shape))
    spots = []
    for shift in (0, 1):
        where = [jax.random.randint(jax.random.fold_in(rng, axis), (), 0, length) for axis, length in enumerate(values.shape)]
        where[longest] = (where[longest] + shift) % values.shape[longest]
        spots.append(tuple(where))
    return values.at[spots[0]].set(low).at[spots[1]].set(high)


def levels(key, shape, shards, low, high):
    def one(position, blocks):
        draws = jax.random.uniform(jax.random.fold_in(jax.random.fold_in(key, 6), position), (blocks,), jnp.float32, low / len(shards), high / len(shards))
        return jnp.repeat(jnp.exp(draws), shape[position] // blocks).reshape((-1,) + (1,) * (len(shape) - position - 1))

    factor_of = one(*shards[0])
    for cut in shards[1:]:
        factor_of = factor_of * one(*cut)
    return factor_of


def normal_values(rng, extent, width, reach, cuts=(), held_as=jnp.bfloat16):
    values = width * jax.random.normal(rng, extent, jnp.float32)
    if cuts:
        values = values * levels(rng, extent, cuts, -0.22, 0.18)
    return jnp.clip(values, -reach, reach).astype(held_as)


def setup_inputs(seed: int = 0) -> dict:
    seeds = jax.random.split(jax.random.key(seed), 6)
    return {
        "queries": draw_queries(jax.random.fold_in(seeds[5], 71), 0),
        "keys": draw_keys(jax.random.fold_in(seeds[5], 71), 0),
        "values": normal_values(seeds[2], (SLOTS, KV_HEADS * HEAD_DIM), 1.0, 6.0, ((0, 512),)),
        "frame_of": jax.random.permutation(seeds[3], FRAMES).astype(jnp.int32),
        "counts": set_ends(jax.random.randint(seeds[4], (FRAMES,), FRAME_TOK // 2, FRAME_TOK + 1), jax.random.fold_in(seeds[4], 1), FRAME_TOK // 2, FRAME_TOK).astype(jnp.int32),
    }


NEGATIVE = -1.0e30


def visible(query_pos, query_tok, key_pos, key_tok, key_count):
    earlier = key_pos[None, :] < query_pos[:, None]
    same_frame = (key_pos[None, :] == query_pos[:, None]) & (key_tok[None, :] <= query_tok[:, None])
    return (earlier | same_frame) & (key_tok < key_count)[None, :]


def reference(queries, keys, values, frame_of, counts):
    group_frames = FRAME_DEV * N_HEAD
    group_rows = group_frames * FRAME_TOK
    group_size = Q_HEADS // KV_HEADS
    slot_pos = jnp.repeat(frame_of, FRAME_TOK).reshape(N_BLK, group_rows)
    slot_count = jnp.repeat(counts, FRAME_TOK).reshape(N_BLK, group_rows)
    query_tok = jnp.arange(group_rows, dtype=jnp.int32) % FRAME_TOK
    key_tok = jnp.tile(query_tok, CYCLE)
    grouped_q = queries.reshape(N_BLK, group_rows, KV_HEADS, group_size, HEAD_DIM)
    grouped_k = keys.reshape(N_BLK, group_rows, KV_HEADS, HEAD_DIM)
    grouped_v = values.reshape(N_BLK, group_rows, KV_HEADS, HEAD_DIM)

    def per_group(group_index):
        sources = (group_index - jnp.arange(CYCLE, dtype=jnp.int32)) % N_BLK
        window_keys = grouped_k[sources].reshape(CYCLE * group_rows, KV_HEADS, HEAD_DIM)
        window_values = grouped_v[sources].reshape(CYCLE * group_rows, KV_HEADS, HEAD_DIM)
        key_pos = slot_pos[sources].reshape(CYCLE * group_rows)
        key_count = slot_count[sources].reshape(CYCLE * group_rows)
        allowed = visible(slot_pos[group_index], query_tok, key_pos, key_tok, key_count)
        scores = jnp.einsum("rcge,kce->cgrk", grouped_q[group_index].astype(jnp.float32),
                            window_keys.astype(jnp.float32), precision=lax.Precision.HIGHEST) * (HEAD_DIM ** -0.5)
        masked = jnp.where(allowed[None, None], scores, NEGATIVE)
        largest = jnp.max(masked, axis=-1, keepdims=True)
        weights = jnp.where(allowed[None, None], jnp.exp(masked - largest), 0.0)
        weight_sum = jnp.sum(weights, axis=-1)
        rounded = lax.optimization_barrier(weights.astype(jnp.bfloat16)).astype(jnp.float32)
        weighted = jnp.einsum("cgrk,kce->cgre", rounded, window_values.astype(jnp.float32),
                              precision=lax.Precision.HIGHEST)
        attended = weighted / weight_sum[..., None]
        return attended.transpose(2, 0, 1, 3).reshape(group_rows, Q_HEADS * HEAD_DIM).astype(jnp.bfloat16)

    result = lax.map(per_group, jnp.arange(N_BLK, dtype=jnp.int32))
    return result.reshape(SLOTS, Q_HEADS * HEAD_DIM)
```

```python
import functools
import math

import jax
import jax.numpy as jnp
from jax import lax
from jax.experimental import pallas as pl
from jax.experimental.pallas import tpu as pltpu
from jax.sharding import PartitionSpec as P

HEAD_DIM = 128
FRAME_TOK = 128
CYCLE = 4
NEGATIVE = -1e30
SCALE = math.log2(math.e) * HEAD_DIM ** (-0.5)

NX, NYLO, NYHI, NZ, NC = 4, 4, 2, 8, 2
AXES = ("blk", "head")


def flat(place):
    x, y, z, c = place
    return ((x * NYLO + y % NYLO) * NZ + z) * (NYHI * NC) + (y // NYLO) * NC + c


def places():
    for x in range(NX):
        for y in range(NYLO * NYHI):
            for z in range(NZ):
                for c in range(NC):
                    yield (x, y, z, c)


def next_group(place):
    x, y, z, c = place
    z += 1
    if z == NZ:
        z = 0
        if y % NYLO == NYLO - 1:
            x = (x + 1) % NX
        y = (y + 1) % (NYLO * NYHI)
    return (x, y, z, c)


def other_column(place):
    x, y, z, c = place
    return (x, (y + NYLO) % (NYLO * NYHI), z, c)


def other_core(place):
    x, y, z, c = place
    return (x, y, z, 1 - c)


def moved(value, target):
    return lax.ppermute(value, AXES, [(flat(p), flat(target(p))) for p in places()])


def attend_kernel(tags, first, last, where_ref, frame_ref, count_ref, query_ref, *refs):
    pieces, refs = refs[: len(tags)], refs[len(tags):]
    if not first:
        (acc_in, stat_in), refs = refs[:2], refs[2:]
    blk, head = where_ref[0], where_ref[1]
    group_dev = NYHI * NC
    blocks = NX * NYLO * NZ
    query_pos = frame_ref[blk * group_dev + head]
    key_tok = lax.broadcasted_iota(jnp.int32, (FRAME_TOK, FRAME_TOK), 0)
    query_tok = lax.broadcasted_iota(jnp.int32, (FRAME_TOK, FRAME_TOK), 1)
    allowed = []
    for offset, column, mate in tags:
        source = lax.rem(blk - offset + blocks, blocks)
        crossed = jnp.where(source // (NYLO * NZ) != blk // (NYLO * NZ), 1, 0)
        side = lax.rem(head // NC + crossed + column, NYHI)
        core = lax.rem(head + mate, NC)
        frame = source * group_dev + side * NC + core
        limit = jnp.where(frame_ref[frame] < query_pos, count_ref[frame], 0)
        if (offset, column, mate) == (0, 0, 0):
            seen = (key_tok <= query_tok) & (key_tok < count_ref[frame])
        else:
            seen = key_tok < limit
        allowed.append(jnp.concatenate([seen] * 4, axis=1))
    allowed = jnp.concatenate(allowed, axis=0) if len(allowed) > 1 else allowed[0]
    kv_heads = pieces[0].shape[1] // (2 * HEAD_DIM)
    for c in range(kv_heads):
        queries = jnp.concatenate(
            [query_ref[:, (4 * c + r) * HEAD_DIM:(4 * c + r + 1) * HEAD_DIM] for r in range(4)], axis=0
        )
        keys = jnp.concatenate([p[:, c * HEAD_DIM:(c + 1) * HEAD_DIM] for p in pieces], axis=0)
        values = jnp.concatenate(
            [p[:, (kv_heads + c) * HEAD_DIM:(kv_heads + c + 1) * HEAD_DIM] for p in pieces], axis=0
        )
        scores = lax.dot_general(
            keys, queries, (((1,), (1,)), ((), ())), preferred_element_type=jnp.float32
        )
        scores = jnp.where(allowed, scores, NEGATIVE)
        top = jnp.max(scores, axis=0, keepdims=True)
        if not first:
            old = stat_in[c:c + 1, :]
            top = jnp.maximum(top, old)
        weights = jnp.exp2((scores - top) * SCALE)
        total = jnp.sum(weights, axis=0, keepdims=True)
        weighted = lax.dot_general(
            values, weights.astype(jnp.bfloat16), (((0,), (0,)), ((), ())),
            preferred_element_type=jnp.float32,
        )
        if not first:
            shrink = jnp.exp2((old - top) * SCALE)
            total = total + stat_in[kv_heads + c:kv_heads + c + 1, :] * shrink
            weighted = weighted + acc_in[c] * shrink
        if last:
            (out_ref,) = refs
            result = weighted / total
            for r in range(4):
                out_ref[:, (4 * c + r) * HEAD_DIM:(4 * c + r + 1) * HEAD_DIM] = (
                    result[:, r * FRAME_TOK:(r + 1) * FRAME_TOK].T.astype(jnp.bfloat16)
                )
        else:
            acc_ref, stat_ref = refs
            acc_ref[c] = weighted
            stat_ref[c:c + 1, :] = top
            stat_ref[kv_heads + c:kv_heads + c + 1, :] = total


def attend(tags, state, last, where, frame_of, counts, queries, pieces):
    rows, width = queries.shape
    kv_heads = pieces[0].shape[1] // (2 * HEAD_DIM)
    in_smem = pl.BlockSpec(memory_space=pltpu.SMEM)
    in_vmem = pl.BlockSpec(memory_space=pltpu.VMEM)
    if last:
        out_shape = jax.ShapeDtypeStruct((rows, width), jnp.bfloat16)
        out_specs = in_vmem
    else:
        out_shape = (
            jax.ShapeDtypeStruct((kv_heads, HEAD_DIM, 4 * FRAME_TOK), jnp.float32),
            jax.ShapeDtypeStruct((2 * kv_heads, 4 * FRAME_TOK), jnp.float32),
        )
        out_specs = (in_vmem, in_vmem)
    keys = len(pieces) * FRAME_TOK
    per_head = 4 * FRAME_TOK * keys
    return pl.pallas_call(
        functools.partial(attend_kernel, tags, state is None, last),
        out_shape=out_shape,
        in_specs=[in_smem] * 3 + [in_vmem] * (1 + len(pieces) + (0 if state is None else 2)),
        out_specs=out_specs,
        compiler_params=pltpu.CompilerParams(vmem_limit_bytes=40 * 1024 * 1024),
        cost_estimate=pl.CostEstimate(
            flops=4 * HEAD_DIM * per_head * kv_heads,
            bytes_accessed=(len(pieces) + 4) * 256 * 1024,
            transcendentals=per_head * kv_heads,
        ),
    )(where, frame_of, counts, queries, *pieces, *(() if state is None else state))


def on_device(queries, keys, values, frame_of, counts):
    where = jnp.stack([lax.axis_index("blk"), lax.axis_index("head")]).astype(jnp.int32)
    own = jnp.concatenate([keys, values], axis=1)
    cross = [moved(own, other_column)]
    near = [own]
    for offset in range(1, CYCLE):
        near.append(moved(near[-1], next_group))
        cross.append(moved(cross[-1], next_group))
    run = functools.partial(attend, where=where, frame_of=frame_of, counts=counts, queries=queries)

    def stage(entries, state, last):
        tags, pieces = [], []
        for offset, column in entries:
            piece = (near, cross)[column][offset]
            tags += [(offset, column, 0), (offset, column, 1)]
            pieces += [piece, moved(piece, other_core)]
        return run(tuple(tags), state, last, pieces=pieces)

    state = stage([(0, 0)], None, False)
    state = stage([(1, 0), (0, 1)], state, False)
    state = stage([(2, 0), (1, 1)], state, False)
    state = stage([(3, 0), (2, 1)], state, False)
    return stage([(3, 1)], state, True)


def solution(mesh):
    in_specs = (
        P(("blk", "head"), None),
        P(("blk", "head"), None),
        P(("blk", "head"), None),
        P(),
        P(),
    )
    out_specs = P(("blk", "head"), None)
    return jax.shard_map(
        on_device, mesh=mesh, in_specs=in_specs, out_specs=out_specs, check_vma=False
    )
```

```python
import functools
import math

import jax
import jax.numpy as jnp
from jax import lax
from jax.experimental import pallas as pl
from jax.experimental.pallas import tpu as pltpu
from jax.sharding import PartitionSpec as P

HEAD_DIM = 128
FRAME_TOK = 128
CYCLE = 4
NEGATIVE = -1e30
SCALE = math.log2(math.e) * HEAD_DIM ** (-0.5)

NX, NYLO, NYHI, NZ, NC = 4, 4, 2, 8, 2
AXES = ("blk", "head")
BLOCKS, GROUP_DEV = NX * NYLO * NZ, NYHI * NC
GROUP = 4


def flat(place):
    x, y, z, c = place
    return ((x * NYLO + y % NYLO) * NZ + z) * (NYHI * NC) + (y // NYLO) * NC + c


def places():
    for x in range(NX):
        for y in range(NYLO * NYHI):
            for z in range(NZ):
                for c in range(NC):
                    yield (x, y, z, c)


def next_group(place):
    x, y, z, c = place
    z += 1
    if z == NZ:
        z = 0
        if y % NYLO == NYLO - 1:
            x = (x + 1) % NX
        y = (y + 1) % (NYLO * NYHI)
    return (x, y, z, c)


def other_column(place):
    x, y, z, c = place
    return (x, (y + NYLO) % (NYLO * NYHI), z, c)


def other_core(place):
    x, y, z, c = place
    return (x, y, z, 1 - c)


def moved(value, target, sources=lambda place: True):
    return lax.ppermute(value, AXES, [(flat(p), flat(target(p))) for p in places() if sources(p)])


def inside(value):
    return moved(value, next_group, lambda place: place[2] != NZ - 1)


def onward(value):
    return moved(value, next_group, lambda place: place[2] == NZ - 1)


def after(value, *others):
    return lax.optimization_barrier((value, *others))[0]


def kv_heads_of(piece):
    return piece.shape[1] // (2 * HEAD_DIM)


def head_rows(query_ref, c):
    return jnp.concatenate(
        [query_ref[:, (GROUP * c + r) * HEAD_DIM:(GROUP * c + r + 1) * HEAD_DIM] for r in range(GROUP)], axis=0
    )


def piece_frame(blk, head, tag):
    offset, column = tag
    source = lax.rem(blk - offset + BLOCKS, BLOCKS)
    crossed = jnp.where(source // (NYLO * NZ) != blk // (NYLO * NZ), 1, 0)
    side = lax.rem(head // NC + crossed + column, NYHI)
    return source * GROUP_DEV + side * NC + lax.rem(head, NC)


def attend_kernel(tags, sets, first, sent, where_ref, frame_ref, count_ref, *refs):
    query_refs, refs = refs[: len(sets)], refs[len(sets):]
    pieces, refs = refs[: len(tags)], refs[len(tags):]
    if first:
        states_in, states_out = None, refs
    else:
        states_in, states_out = refs[: 2 * len(sets)], refs[2 * len(sets):]
    blk, head = where_ref[0], where_ref[1]
    kv_heads = kv_heads_of(pieces[0])
    rows = GROUP * FRAME_TOK
    key_tok = lax.broadcasted_iota(jnp.int32, (FRAME_TOK, rows), 0)
    query_tok = lax.rem(lax.broadcasted_iota(jnp.int32, (FRAME_TOK, rows), 1), FRAME_TOK)
    allowed = []
    for mate in sets:
        core = lax.rem(head + mate, NC)
        query_pos = frame_ref[blk * GROUP_DEV + head - lax.rem(head, NC) + core]
        parts = []
        for tag in tags:
            frame = piece_frame(blk, head, tag)
            if tag == (0, 0) and mate == 0:
                parts.append((key_tok <= query_tok) & (key_tok < count_ref[frame]))
            else:
                limit = jnp.where(frame_ref[frame] < query_pos, count_ref[frame], 0)
                parts.append(key_tok < limit)
        allowed.append(parts)
    stats = []
    todo = [(i, c) for i in range(len(sets)) for c in range(kv_heads)]

    def score(i, c):
        keys = [p[:, c * HEAD_DIM:(c + 1) * HEAD_DIM] for p in pieces]
        scores = lax.dot_general(
            jnp.concatenate(keys, axis=0) if len(keys) > 1 else keys[0], head_rows(query_refs[i], c),
            (((1,), (1,)), ((), ())), preferred_element_type=jnp.float32,
        )
        masked = [
            jnp.where(allowed[i][f], scores[f * FRAME_TOK:(f + 1) * FRAME_TOK], NEGATIVE) for f in range(len(tags))
        ]
        return jnp.concatenate(masked, axis=0) if len(masked) > 1 else masked[0]

    def weigh(i, c, scores):
        top = jnp.max(scores, axis=0, keepdims=True)
        shrink = None
        if not first:
            stat = states_in[2 * i + 1]
            old = stat[c:c + 1, :]
            top = jnp.maximum(top, old)
            shrink = jnp.exp2((old - top) * SCALE)
        weights = jnp.exp2((scores - top) * SCALE)
        total = jnp.sum(weights, axis=0, keepdims=True)
        if not first:
            total = total + stat[kv_heads + c:kv_heads + c + 1, :] * shrink
        return weights.astype(jnp.bfloat16), top, total, shrink

    def gather(i, c, weights, top, total, shrink):
        values = [p[:, (kv_heads + c) * HEAD_DIM:(kv_heads + c + 1) * HEAD_DIM] for p in pieces]
        weighted = lax.dot_general(
            jnp.concatenate(values, axis=0) if len(values) > 1 else values[0], weights,
            (((0,), (0,)), ((), ())), preferred_element_type=jnp.float32,
        )
        if not first:
            weighted = weighted + states_in[2 * i][c] * shrink
        if sent:
            states_out[0][c * HEAD_DIM:(c + 1) * HEAD_DIM, :] = weighted.astype(jnp.bfloat16)
            stats.append((top, total))
        else:
            states_out[2 * i][c] = weighted
            states_out[2 * i + 1][c:c + 1, :] = top
            states_out[2 * i + 1][kv_heads + c:kv_heads + c + 1, :] = total

    scores = score(*todo[0])
    before = None
    for n, item in enumerate(todo):
        following = score(*todo[n + 1]) if n + 1 < len(todo) else None
        done = weigh(*item, scores)
        if before is not None:
            gather(*todo[n - 1], *before)
        scores, before = following, done
    gather(*todo[-1], *before)
    if sent:
        rest = jnp.concatenate([top for top, _ in stats] + [total for _, total in stats], axis=0)
        parts = []
        for _ in range(3):
            parts.append(rest.astype(jnp.bfloat16).astype(jnp.float32))
            rest = rest - parts[-1]
        packed = jnp.concatenate(parts + [jnp.zeros_like(rest)], axis=0)
        states_out[0][kv_heads * HEAD_DIM:, :] = packed.astype(jnp.bfloat16)


def merge_kernel(acc_ref, stat_ref, got_ref, out_ref):
    kv_heads = acc_ref.shape[0]
    wide = kv_heads * HEAD_DIM
    parts = got_ref[wide:wide + 32, :].astype(jnp.float32)
    got_stat = parts[:8] + parts[8:16] + parts[16:24]
    for c in range(kv_heads):
        top, total = stat_ref[c:c + 1, :], stat_ref[kv_heads + c:kv_heads + c + 1, :]
        got_top, got_total = got_stat[c:c + 1, :], got_stat[kv_heads + c:kv_heads + c + 1, :]
        most = jnp.maximum(top, got_top)
        mine, theirs = jnp.exp2((top - most) * SCALE), jnp.exp2((got_top - most) * SCALE)
        share = 1.0 / (total * mine + got_total * theirs)
        result = acc_ref[c] * (mine * share) + got_ref[c * HEAD_DIM:(c + 1) * HEAD_DIM, :].astype(jnp.float32) * (theirs * share)
        for r in range(GROUP):
            out_ref[:, (GROUP * c + r) * HEAD_DIM:(GROUP * c + r + 1) * HEAD_DIM] = (
                result[:, r * FRAME_TOK:(r + 1) * FRAME_TOK].T.astype(jnp.bfloat16)
            )


IN_SMEM = pl.BlockSpec(memory_space=pltpu.SMEM)
IN_VMEM = pl.BlockSpec(memory_space=pltpu.VMEM)
PARAMS = pltpu.CompilerParams(vmem_limit_bytes=48 * 1024 * 1024)


def attend(tags, sets, state, tables, queries, pieces, sent=False):
    kv_heads = kv_heads_of(pieces[0])
    rows = GROUP * FRAME_TOK
    out_shape = (
        jax.ShapeDtypeStruct((kv_heads, HEAD_DIM, rows), jnp.float32),
        jax.ShapeDtypeStruct((2 * kv_heads, rows), jnp.float32),
    ) * len(sets)
    if sent:
        out_shape = jax.ShapeDtypeStruct((kv_heads * HEAD_DIM + 32, rows), jnp.bfloat16)
    scores = rows * len(pieces) * FRAME_TOK * kv_heads * len(sets)
    return pl.pallas_call(
        functools.partial(attend_kernel, tags, sets, state is None, sent),
        out_shape=out_shape,
        in_specs=[IN_SMEM] * 3 + [IN_VMEM] * (len(sets) + len(pieces) + (0 if state is None else 2 * len(sets))),
        out_specs=IN_VMEM if sent else (IN_VMEM,) * (2 * len(sets)),
        compiler_params=PARAMS,
        cost_estimate=pl.CostEstimate(
            flops=4 * HEAD_DIM * scores, bytes_accessed=1024 * 1024, transcendentals=scores
        ),
    )(*tables, *queries, *pieces, *(() if state is None else state))


def merge(state, got, shape):
    return pl.pallas_call(
        merge_kernel,
        out_shape=jax.ShapeDtypeStruct(shape, jnp.bfloat16),
        in_specs=[IN_VMEM] * 3,
        out_specs=IN_VMEM,
        compiler_params=PARAMS,
        cost_estimate=pl.CostEstimate(flops=4 * shape[0] * shape[1], bytes_accessed=3 * 1024 * 1024, transcendentals=0),
    )(*state, got)


def on_device(queries, keys, values, frame_of, counts):
    blk = lax.axis_index("blk")
    where = jnp.stack([blk, lax.axis_index("head")]).astype(jnp.int32)
    starts_line = lax.rem(blk, NZ) == 0
    tables = (where, frame_of, counts)

    def either(first, other):
        return jnp.where(starts_line, first, other)

    own = jnp.concatenate([keys, values], axis=1)
    cross0 = moved(own, other_column)
    near1 = moved(own, next_group)
    both = (queries, moved(after(queries, near1), other_core))

    in_cross1, on_cross1 = inside(cross0), onward(cross0)
    near2 = moved(near1, next_group)
    state = attend(((0, 0), (0, 1), (1, 0)), (0, 1), None, tables, both, (own, cross0, near1))

    on_cross2 = onward(in_cross1)
    cross1 = either(on_cross1, in_cross1)
    in_cross2 = inside(after(cross1, state[1]))
    near3 = moved(near2, next_group)
    state = attend(((1, 1), (2, 0)), (0, 1), state, tables, both, (cross1, near2))

    on_cross3 = onward(in_cross2)
    cross2 = either(on_cross2, in_cross2)
    in_cross3 = inside(after(cross2, state[1]))
    state = attend(((2, 1), (3, 0)), (0, 1), state, tables, both, (cross2, near3))

    cross3 = either(on_cross3, in_cross3)
    got = moved(attend(((3, 1),), (1,), state[2:], tables, both[1:], (cross3,), True), other_core)
    own_state = attend(((3, 1),), (0,), state[:2], tables, both[:1], (cross3,))
    return merge(own_state, got, queries.shape)


def solution(mesh):
    in_specs = (
        P(("blk", "head"), None),
        P(("blk", "head"), None),
        P(("blk", "head"), None),
        P(),
        P(),
    )
    out_specs = P(("blk", "head"), None)
    return jax.shard_map(
        on_device, mesh=mesh, in_specs=in_specs, out_specs=out_specs, check_vma=False
    )
```

```python
import functools
import math

import jax
import jax.numpy as jnp
from jax import lax
from jax.experimental import pallas as pl
from jax.experimental.pallas import tpu as pltpu
from jax.sharding import PartitionSpec as P

HEAD_DIM = 128
FRAME_TOK = 128
CYCLE = 4
NEGATIVE = -1e30
SCALE = math.log2(math.e) * HEAD_DIM ** (-0.5)

NX, NYLO, NYHI, NZ, NC = 4, 4, 2, 8, 2
AXES = ("blk", "head")
BLOCKS, GROUP_DEV = NX * NYLO * NZ, NYHI * NC
GROUP = 4


def flat(place):
    x, y, z, c = place
    return ((x * NYLO + y % NYLO) * NZ + z) * (NYHI * NC) + (y // NYLO) * NC + c


def places():
    for x in range(NX):
        for y in range(NYLO * NYHI):
            for z in range(NZ):
                for c in range(NC):
                    yield (x, y, z, c)


def next_group(place):
    x, y, z, c = place
    z += 1
    if z == NZ:
        z = 0
        if y % NYLO == NYLO - 1:
            x = (x + 1) % NX
        y = (y + 1) % (NYLO * NYHI)
    return (x, y, z, c)


def other_column(place):
    x, y, z, c = place
    return (x, (y + NYLO) % (NYLO * NYHI), z, c)


def other_core(place):
    x, y, z, c = place
    return (x, y, z, 1 - c)


def moved(value, target, sources=lambda place: True):
    return lax.ppermute(value, AXES, [(flat(p), flat(target(p))) for p in places() if sources(p)])


def inside(value):
    return moved(value, next_group, lambda place: place[2] != NZ - 1)


def onward(value):
    return moved(value, next_group, lambda place: place[2] == NZ - 1)


def after(value, *others):
    return lax.optimization_barrier((value, *others))[0]


def kv_heads_of(piece):
    return piece.shape[1] // (2 * HEAD_DIM)


def head_rows(query_ref, c):
    return jnp.concatenate(
        [query_ref[:, (GROUP * c + r) * HEAD_DIM:(GROUP * c + r + 1) * HEAD_DIM] for r in range(GROUP)], axis=0
    )


def piece_frame(blk, head, tag):
    offset, column = tag
    source = lax.rem(blk - offset + BLOCKS, BLOCKS)
    crossed = jnp.where(source // (NYLO * NZ) != blk // (NYLO * NZ), 1, 0)
    side = lax.rem(head // NC + crossed + column, NYHI)
    return source * GROUP_DEV + side * NC + lax.rem(head, NC)


def attend_kernel(tags, sets, first, sent, where_ref, frame_ref, count_ref, *refs):
    query_refs, refs = refs[: len(sets)], refs[len(sets):]
    pieces, refs = refs[: len(tags)], refs[len(tags):]
    if first:
        states_in, states_out = None, refs
    else:
        states_in, states_out = refs[: 2 * len(sets)], refs[2 * len(sets):]
    blk, head = where_ref[0], where_ref[1]
    kv_heads = kv_heads_of(pieces[0])
    rows = GROUP * FRAME_TOK
    key_tok = lax.broadcasted_iota(jnp.int32, (FRAME_TOK, rows), 0)
    query_tok = lax.rem(lax.broadcasted_iota(jnp.int32, (FRAME_TOK, rows), 1), FRAME_TOK)
    allowed = []
    for mate in sets:
        core = lax.rem(head + mate, NC)
        query_pos = frame_ref[blk * GROUP_DEV + head - lax.rem(head, NC) + core]
        parts = []
        for tag in tags:
            frame = piece_frame(blk, head, tag)
            if tag == (0, 0) and mate == 0:
                parts.append((key_tok <= query_tok) & (key_tok < count_ref[frame]))
            else:
                limit = jnp.where(frame_ref[frame] < query_pos, count_ref[frame], 0)
                parts.append(key_tok < limit)
        allowed.append(parts)
    stats = []
    todo = [(i, c) for i in range(len(sets)) for c in range(kv_heads)]

    def score(i, c):
        keys = [p[:, c * HEAD_DIM:(c + 1) * HEAD_DIM] for p in pieces]
        scores = lax.dot_general(
            jnp.concatenate(keys, axis=0) if len(keys) > 1 else keys[0], head_rows(query_refs[i], c),
            (((1,), (1,)), ((), ())), preferred_element_type=jnp.float32,
        )
        masked = [
            jnp.where(allowed[i][f], scores[f * FRAME_TOK:(f + 1) * FRAME_TOK], NEGATIVE) for f in range(len(tags))
        ]
        return jnp.concatenate(masked, axis=0) if len(masked) > 1 else masked[0]

    def weigh(i, c, scores):
        top = jnp.max(scores, axis=0, keepdims=True)
        shrink = None
        if not first:
            stat = states_in[2 * i + 1]
            old = stat[c:c + 1, :]
            top = jnp.maximum(top, old)
            shrink = jnp.exp2((old - top) * SCALE)
        weights = jnp.exp2((scores - top) * SCALE)
        total = jnp.sum(weights, axis=0, keepdims=True)
        if not first:
            total = total + stat[kv_heads + c:kv_heads + c + 1, :] * shrink
        return weights.astype(jnp.bfloat16), top, total, shrink

    def gather(i, c, weights, top, total, shrink):
        values = [p[:, (kv_heads + c) * HEAD_DIM:(kv_heads + c + 1) * HEAD_DIM] for p in pieces]
        weighted = lax.dot_general(
            jnp.concatenate(values, axis=0) if len(values) > 1 else values[0], weights,
            (((0,), (0,)), ((), ())), preferred_element_type=jnp.float32,
        )
        if not first:
            weighted = weighted + states_in[2 * i][c] * shrink
        if sent:
            states_out[0][c * HEAD_DIM:(c + 1) * HEAD_DIM, :] = weighted.astype(jnp.bfloat16)
            stats.append((top, total))
        else:
            states_out[2 * i][c] = weighted
            states_out[2 * i + 1][c:c + 1, :] = top
            states_out[2 * i + 1][kv_heads + c:kv_heads + c + 1, :] = total

    scores = score(*todo[0])
    before = None
    for n, item in enumerate(todo):
        following = score(*todo[n + 1]) if n + 1 < len(todo) else None
        done = weigh(*item, scores)
        if before is not None:
            gather(*todo[n - 1], *before)
        scores, before = following, done
    gather(*todo[-1], *before)
    if sent:
        rest = jnp.concatenate([top for top, _ in stats] + [total for _, total in stats], axis=0)
        parts = []
        for _ in range(3):
            parts.append(rest.astype(jnp.bfloat16).astype(jnp.float32))
            rest = rest - parts[-1]
        packed = jnp.concatenate(parts + [jnp.zeros_like(rest)], axis=0)
        states_out[0][kv_heads * HEAD_DIM:, :] = packed.astype(jnp.bfloat16)


def merge_kernel(acc_ref, stat_ref, got_ref, out_ref):
    kv_heads = acc_ref.shape[0]
    wide = kv_heads * HEAD_DIM
    parts = got_ref[wide:wide + 32, :].astype(jnp.float32)
    got_stat = parts[:8] + parts[8:16] + parts[16:24]
    for c in range(kv_heads):
        top, total = stat_ref[c:c + 1, :], stat_ref[kv_heads + c:kv_heads + c + 1, :]
        got_top, got_total = got_stat[c:c + 1, :], got_stat[kv_heads + c:kv_heads + c + 1, :]
        most = jnp.maximum(top, got_top)
        mine, theirs = jnp.exp2((top - most) * SCALE), jnp.exp2((got_top - most) * SCALE)
        share = 1.0 / (total * mine + got_total * theirs)
        result = acc_ref[c] * (mine * share) + got_ref[c * HEAD_DIM:(c + 1) * HEAD_DIM, :].astype(jnp.float32) * (theirs * share)
        for r in range(GROUP):
            out_ref[:, (GROUP * c + r) * HEAD_DIM:(GROUP * c + r + 1) * HEAD_DIM] = (
                result[:, r * FRAME_TOK:(r + 1) * FRAME_TOK].T.astype(jnp.bfloat16)
            )


IN_SMEM = pl.BlockSpec(memory_space=pltpu.SMEM)
IN_VMEM = pl.BlockSpec(memory_space=pltpu.VMEM)
PARAMS = pltpu.CompilerParams(vmem_limit_bytes=48 * 1024 * 1024)


def attend(tags, sets, state, tables, queries, pieces, sent=False):
    kv_heads = kv_heads_of(pieces[0])
    rows = GROUP * FRAME_TOK
    out_shape = (
        jax.ShapeDtypeStruct((kv_heads, HEAD_DIM, rows), jnp.float32),
        jax.ShapeDtypeStruct((2 * kv_heads, rows), jnp.float32),
    ) * len(sets)
    if sent:
        out_shape = jax.ShapeDtypeStruct((kv_heads * HEAD_DIM + 32, rows), jnp.bfloat16)
    scores = rows * len(pieces) * FRAME_TOK * kv_heads * len(sets)
    return pl.pallas_call(
        functools.partial(attend_kernel, tags, sets, state is None, sent),
        out_shape=out_shape,
        in_specs=[IN_SMEM] * 3 + [IN_VMEM] * (len(sets) + len(pieces) + (0 if state is None else 2 * len(sets))),
        out_specs=IN_VMEM if sent else (IN_VMEM,) * (2 * len(sets)),
        compiler_params=PARAMS,
        cost_estimate=pl.CostEstimate(
            flops=4 * HEAD_DIM * scores, bytes_accessed=1024 * 1024, transcendentals=scores
        ),
    )(*tables, *queries, *pieces, *(() if state is None else state))


def merge(state, got, shape):
    return pl.pallas_call(
        merge_kernel,
        out_shape=jax.ShapeDtypeStruct(shape, jnp.bfloat16),
        in_specs=[IN_VMEM] * 3,
        out_specs=IN_VMEM,
        compiler_params=PARAMS,
        cost_estimate=pl.CostEstimate(flops=4 * shape[0] * shape[1], bytes_accessed=3 * 1024 * 1024, transcendentals=0),
    )(*state, got)


def on_device(queries, keys, values, frame_of, counts):
    blk = lax.axis_index("blk")
    where = jnp.stack([blk, lax.axis_index("head")]).astype(jnp.int32)
    starts_line = lax.rem(blk, NZ) == 0
    tables = (where, frame_of, counts)

    def either(first, other):
        return jnp.where(starts_line, first, other)

    own = jnp.concatenate([keys, values], axis=1)
    rows = own.shape[0]
    near1 = moved(own, next_group)
    cross0 = moved(own, other_column)
    in_near2 = inside(near1)
    both = (queries, moved(after(queries, near1), other_core))
    on_first = onward(jnp.concatenate([cross0, near1], axis=0))
    in_cross1 = inside(after(cross0, in_near2))
    on_second = onward(jnp.concatenate([in_cross1, in_near2], axis=0))
    cross1, near2 = either(on_first[:rows], in_cross1), either(on_first[rows:], in_near2)
    state = attend(((0, 0), (0, 1), (1, 0)), (0, 1), None, tables, both, (own, cross0, near1))
    in_cross2 = inside(after(cross1, state[1]))
    in_near3 = inside(near2)
    on_cross3 = onward(in_cross2)
    cross2, near3 = either(on_second[:rows], in_cross2), either(on_second[rows:], in_near3)
    in_cross3 = inside(cross2)
    state = attend(((2, 0), (1, 1), (3, 0), (2, 1)), (0, 1), state, tables, both, (near2, cross1, near3, cross2))
    cross3 = either(on_cross3, in_cross3)
    got = moved(attend(((3, 1),), (1,), state[2:], tables, both[1:], (cross3,), True), other_core)
    own_state = attend(((3, 1),), (0,), state[:2], tables, both[:1], (cross3,))
    return merge(own_state, got, queries.shape)


def solution(mesh):
    in_specs = (
        P(("blk", "head"), None),
        P(("blk", "head"), None),
        P(("blk", "head"), None),
        P(),
        P(),
    )
    out_specs = P(("blk", "head"), None)
    return jax.shard_map(
        on_device, mesh=mesh, in_specs=in_specs, out_specs=out_specs, check_vma=False
    )
```

```python
import functools
import math

import jax
import jax.numpy as jnp
from jax import lax
from jax.experimental import pallas as pl
from jax.experimental.pallas import tpu as pltpu
from jax.sharding import PartitionSpec as P

HEAD_DIM = 128
FRAME_TOK = 128
CYCLE = 4
NEGATIVE = -1e30
SCALE = math.log2(math.e) * HEAD_DIM ** (-0.5)

NX, NYLO, NYHI, NZ, NC = 4, 4, 2, 8, 2
AXES = ("blk", "head")
BLOCKS, GROUP_DEV = NX * NYLO * NZ, NYHI * NC
GROUP = 4


def flat(place):
    x, y, z, c = place
    return ((x * NYLO + y % NYLO) * NZ + z) * (NYHI * NC) + (y // NYLO) * NC + c


def places():
    for x in range(NX):
        for y in range(NYLO * NYHI):
            for z in range(NZ):
                for c in range(NC):
                    yield (x, y, z, c)


def next_group(place):
    x, y, z, c = place
    z += 1
    if z == NZ:
        z = 0
        if y % NYLO == NYLO - 1:
            x = (x + 1) % NX
        y = (y + 1) % (NYLO * NYHI)
    return (x, y, z, c)


def other_column(place):
    x, y, z, c = place
    return (x, (y + NYLO) % (NYLO * NYHI), z, c)


def other_core(place):
    x, y, z, c = place
    return (x, y, z, 1 - c)


def moved(value, target, sources=lambda place: True):
    return lax.ppermute(value, AXES, [(flat(p), flat(target(p))) for p in places() if sources(p)])


def inside(value):
    return moved(value, next_group, lambda place: place[2] != NZ - 1)


def onward(value):
    return moved(value, next_group, lambda place: place[2] == NZ - 1)


def after(value, *others):
    return lax.optimization_barrier((value, *others))[0]


def kv_heads_of(piece):
    return piece.shape[1] // (2 * HEAD_DIM)


def head_rows(query_ref, c):
    return jnp.concatenate(
        [query_ref[:, (GROUP * c + r) * HEAD_DIM:(GROUP * c + r + 1) * HEAD_DIM] for r in range(GROUP)], axis=0
    )


def piece_frame(blk, head, tag):
    offset, column = tag
    source = lax.rem(blk - offset + BLOCKS, BLOCKS)
    crossed = jnp.where(source // (NYLO * NZ) != blk // (NYLO * NZ), 1, 0)
    side = lax.rem(head // NC + crossed + column, NYHI)
    return source * GROUP_DEV + side * NC + lax.rem(head, NC)


def attend_kernel(tags, sets, first, sent, where_ref, frame_ref, count_ref, *refs):
    query_refs, refs = refs[: len(sets)], refs[len(sets):]
    pieces, refs = refs[: len(tags)], refs[len(tags):]
    if first:
        states_in, states_out = None, refs
    else:
        states_in, states_out = refs[: 2 * len(sets)], refs[2 * len(sets):]
    blk, head = where_ref[0], where_ref[1]
    kv_heads = kv_heads_of(pieces[0])
    rows = GROUP * FRAME_TOK
    key_tok = lax.broadcasted_iota(jnp.int32, (FRAME_TOK, rows), 0)
    query_tok = lax.rem(lax.broadcasted_iota(jnp.int32, (FRAME_TOK, rows), 1), FRAME_TOK)
    allowed = []
    for mate in sets:
        core = lax.rem(head + mate, NC)
        query_pos = frame_ref[blk * GROUP_DEV + head - lax.rem(head, NC) + core]
        parts = []
        for tag in tags:
            frame = piece_frame(blk, head, tag)
            if tag == (0, 0) and mate == 0:
                parts.append((key_tok <= query_tok) & (key_tok < count_ref[frame]))
            else:
                limit = jnp.where(frame_ref[frame] < query_pos, count_ref[frame], 0)
                parts.append(key_tok < limit)
        allowed.append(parts)
    stats = []
    todo = [(i, c) for i in range(len(sets)) for c in range(kv_heads)]

    def score(i, c):
        keys = [p[:, c * HEAD_DIM:(c + 1) * HEAD_DIM] for p in pieces]
        scores = lax.dot_general(
            jnp.concatenate(keys, axis=0) if len(keys) > 1 else keys[0], head_rows(query_refs[i], c),
            (((1,), (1,)), ((), ())), preferred_element_type=jnp.float32,
        )
        masked = [
            jnp.where(allowed[i][f], scores[f * FRAME_TOK:(f + 1) * FRAME_TOK], NEGATIVE) for f in range(len(tags))
        ]
        return jnp.concatenate(masked, axis=0) if len(masked) > 1 else masked[0]

    def weigh(i, c, scores):
        top = jnp.max(scores, axis=0, keepdims=True)
        shrink = None
        if not first:
            stat = states_in[2 * i + 1]
            old = stat[c:c + 1, :]
            top = jnp.maximum(top, old)
            shrink = jnp.exp2((old - top) * SCALE)
        weights = jnp.exp2((scores - top) * SCALE)
        total = jnp.sum(weights, axis=0, keepdims=True)
        if not first:
            total = total + stat[kv_heads + c:kv_heads + c + 1, :] * shrink
        return weights.astype(jnp.bfloat16), top, total, shrink

    def gather(i, c, weights, top, total, shrink):
        values = [p[:, (kv_heads + c) * HEAD_DIM:(kv_heads + c + 1) * HEAD_DIM] for p in pieces]
        weighted = lax.dot_general(
            jnp.concatenate(values, axis=0) if len(values) > 1 else values[0], weights,
            (((0,), (0,)), ((), ())), preferred_element_type=jnp.float32,
        )
        if not first:
            weighted = weighted + states_in[2 * i][c] * shrink
        if sent:
            states_out[0][c * HEAD_DIM:(c + 1) * HEAD_DIM, :] = weighted.astype(jnp.bfloat16)
            stats.append((top, total))
        else:
            states_out[2 * i][c] = weighted
            states_out[2 * i + 1][c:c + 1, :] = top
            states_out[2 * i + 1][kv_heads + c:kv_heads + c + 1, :] = total

    scores = score(*todo[0])
    before = None
    for n, item in enumerate(todo):
        following = score(*todo[n + 1]) if n + 1 < len(todo) else None
        done = weigh(*item, scores)
        if before is not None:
            gather(*todo[n - 1], *before)
        scores, before = following, done
    gather(*todo[-1], *before)
    if sent:
        rest = jnp.concatenate([top for top, _ in stats] + [total for _, total in stats], axis=0)
        parts = []
        for _ in range(3):
            parts.append(rest.astype(jnp.bfloat16).astype(jnp.float32))
            rest = rest - parts[-1]
        packed = jnp.concatenate(parts + [jnp.zeros_like(rest)], axis=0)
        states_out[0][kv_heads * HEAD_DIM:, :] = packed.astype(jnp.bfloat16)


def merge_kernel(acc_ref, stat_ref, got_ref, out_ref):
    kv_heads = acc_ref.shape[0]
    wide = kv_heads * HEAD_DIM
    parts = got_ref[wide:wide + 32, :].astype(jnp.float32)
    got_stat = parts[:8] + parts[8:16] + parts[16:24]
    for c in range(kv_heads):
        top, total = stat_ref[c:c + 1, :], stat_ref[kv_heads + c:kv_heads + c + 1, :]
        got_top, got_total = got_stat[c:c + 1, :], got_stat[kv_heads + c:kv_heads + c + 1, :]
        most = jnp.maximum(top, got_top)
        mine, theirs = jnp.exp2((top - most) * SCALE), jnp.exp2((got_top - most) * SCALE)
        share = 1.0 / (total * mine + got_total * theirs)
        result = acc_ref[c] * (mine * share) + got_ref[c * HEAD_DIM:(c + 1) * HEAD_DIM, :].astype(jnp.float32) * (theirs * share)
        for r in range(GROUP):
            out_ref[:, (GROUP * c + r) * HEAD_DIM:(GROUP * c + r + 1) * HEAD_DIM] = (
                result[:, r * FRAME_TOK:(r + 1) * FRAME_TOK].T.astype(jnp.bfloat16)
            )


IN_SMEM = pl.BlockSpec(memory_space=pltpu.SMEM)
IN_VMEM = pl.BlockSpec(memory_space=pltpu.VMEM)
PARAMS = pltpu.CompilerParams(vmem_limit_bytes=20 * 1024 * 1024)


def attend(tags, sets, state, tables, queries, pieces, sent=False):
    kv_heads = kv_heads_of(pieces[0])
    rows = GROUP * FRAME_TOK
    out_shape = (
        jax.ShapeDtypeStruct((kv_heads, HEAD_DIM, rows), jnp.float32),
        jax.ShapeDtypeStruct((2 * kv_heads, rows), jnp.float32),
    ) * len(sets)
    if sent:
        out_shape = jax.ShapeDtypeStruct((kv_heads * HEAD_DIM + 32, rows), jnp.bfloat16)
    scores = rows * len(pieces) * FRAME_TOK * kv_heads * len(sets)
    return pl.pallas_call(
        functools.partial(attend_kernel, tags, sets, state is None, sent),
        out_shape=out_shape,
        in_specs=[IN_SMEM] * 3 + [IN_VMEM] * (len(sets) + len(pieces) + (0 if state is None else 2 * len(sets))),
        out_specs=IN_VMEM if sent else (IN_VMEM,) * (2 * len(sets)),
        compiler_params=PARAMS,
        cost_estimate=pl.CostEstimate(
            flops=4 * HEAD_DIM * scores, bytes_accessed=1024 * 1024, transcendentals=scores
        ),
    )(*tables, *queries, *pieces, *(() if state is None else state))


def merge(state, got, shape):
    return pl.pallas_call(
        merge_kernel,
        out_shape=jax.ShapeDtypeStruct(shape, jnp.bfloat16),
        in_specs=[IN_VMEM] * 3,
        out_specs=IN_VMEM,
        compiler_params=PARAMS,
        cost_estimate=pl.CostEstimate(flops=4 * shape[0] * shape[1], bytes_accessed=3 * 1024 * 1024, transcendentals=0),
    )(*state, got)


def on_device(queries, keys, values, frame_of, counts):
    blk = lax.axis_index("blk")
    where = jnp.stack([blk, lax.axis_index("head")]).astype(jnp.int32)
    starts_line = lax.rem(blk, NZ) == 0
    tables = (where, frame_of, counts)

    def either(first, other):
        return jnp.where(starts_line, first, other)

    own = jnp.concatenate([keys, values], axis=1)
    rows = own.shape[0]
    near1 = moved(own, next_group)
    cross0 = moved(own, other_column)
    in_near2 = inside(near1)
    both = (queries, moved(after(queries, near1), other_core))
    on_first = onward(jnp.concatenate([cross0, near1], axis=0))
    in_cross1 = inside(after(cross0, in_near2))
    on_second = onward(jnp.concatenate([in_cross1, in_near2], axis=0))
    cross1, near2 = either(on_first[:rows], in_cross1), either(on_first[rows:], in_near2)
    state = attend(((0, 0), (0, 1), (1, 0)), (0, 1), None, tables, both, (own, cross0, near1))
    in_cross2 = inside(after(cross1, state[1]))
    in_near3 = inside(near2)
    on_cross3 = onward(in_cross2)
    cross2 = either(on_second[:rows], in_cross2)
    in_cross3 = inside(cross2)
    near3 = either(after(on_second, cross2)[rows:], in_near3)
    state = attend(((2, 0), (1, 1), (3, 0), (2, 1)), (0, 1), state, tables, both, (near2, cross1, near3, cross2))
    cross3 = either(on_cross3, in_cross3)
    got = moved(attend(((3, 1),), (1,), state[2:], tables, both[1:], (cross3,), True), other_core)
    own_state = attend(((3, 1),), (0,), state[:2], tables, both[:1], (cross3,))
    return merge(own_state, got, queries.shape)


def solution(mesh):
    in_specs = (
        P(("blk", "head"), None),
        P(("blk", "head"), None),
        P(("blk", "head"), None),
        P(),
        P(),
    )
    out_specs = P(("blk", "head"), None)
    return jax.shard_map(
        on_device, mesh=mesh, in_specs=in_specs, out_specs=out_specs, check_vma=False
    )
```

```python
import functools
import math

import jax
import jax.numpy as jnp
from jax import lax
from jax.experimental import pallas as pl
from jax.experimental.pallas import tpu as pltpu
from jax.sharding import PartitionSpec as P

HEAD_DIM = 128
FRAME_TOK = 128
CYCLE = 4
NEGATIVE = -1e30
SCALE = math.log2(math.e) * HEAD_DIM ** (-0.5)

NX, NYLO, NYHI, NZ, NC = 4, 4, 2, 8, 2
AXES = ("blk", "head")
BLOCKS, GROUP_DEV = NX * NYLO * NZ, NYHI * NC
GROUP = 4


def flat(place):
    x, y, z, c = place
    return ((x * NYLO + y % NYLO) * NZ + z) * (NYHI * NC) + (y // NYLO) * NC + c


def places():
    for x in range(NX):
        for y in range(NYLO * NYHI):
            for z in range(NZ):
                for c in range(NC):
                    yield (x, y, z, c)


def next_group(place):
    x, y, z, c = place
    z += 1
    if z == NZ:
        z = 0
        if y % NYLO == NYLO - 1:
            x = (x + 1) % NX
        y = (y + 1) % (NYLO * NYHI)
    return (x, y, z, c)


def other_column(place):
    x, y, z, c = place
    return (x, (y + NYLO) % (NYLO * NYHI), z, c)


def other_core(place):
    x, y, z, c = place
    return (x, y, z, 1 - c)


def moved(value, target, sources=lambda place: True):
    return lax.ppermute(value, AXES, [(flat(p), flat(target(p))) for p in places() if sources(p)])


def inside(value):
    return moved(value, next_group, lambda place: place[2] != NZ - 1)


def onward(value):
    return moved(value, next_group, lambda place: place[2] == NZ - 1)


def after(value, *others):
    return lax.optimization_barrier((value, *others))[0]


def kv_heads_of(piece):
    return piece.shape[1] // (2 * HEAD_DIM)


def head_rows(query_ref, c):
    return jnp.concatenate(
        [query_ref[:, (GROUP * c + r) * HEAD_DIM:(GROUP * c + r + 1) * HEAD_DIM] for r in range(GROUP)], axis=0
    )


def piece_frame(blk, head, tag):
    offset, column = tag
    source = lax.rem(blk - offset + BLOCKS, BLOCKS)
    crossed = jnp.where(source // (NYLO * NZ) != blk // (NYLO * NZ), 1, 0)
    side = lax.rem(head // NC + crossed + column, NYHI)
    return source * GROUP_DEV + side * NC + lax.rem(head, NC)


def attend_kernel(tags, sets, first, sent, where_ref, frame_ref, count_ref, *refs):
    query_refs, refs = refs[: len(sets)], refs[len(sets):]
    pieces, refs = refs[: len(tags)], refs[len(tags):]
    if first:
        states_in, states_out = None, refs
    else:
        states_in, states_out = refs[: 2 * len(sets)], refs[2 * len(sets):]
    blk, head = where_ref[0], where_ref[1]
    kv_heads = kv_heads_of(pieces[0])
    rows = GROUP * FRAME_TOK
    key_tok = lax.broadcasted_iota(jnp.int32, (FRAME_TOK, rows), 0)
    query_tok = lax.rem(lax.broadcasted_iota(jnp.int32, (FRAME_TOK, rows), 1), FRAME_TOK)
    allowed = []
    for mate in sets:
        core = lax.rem(head + mate, NC)
        query_pos = frame_ref[blk * GROUP_DEV + head - lax.rem(head, NC) + core]
        parts = []
        for tag in tags:
            frame = piece_frame(blk, head, tag)
            if tag == (0, 0) and mate == 0:
                parts.append((key_tok <= query_tok) & (key_tok < count_ref[frame]))
            else:
                limit = jnp.where(frame_ref[frame] < query_pos, count_ref[frame], 0)
                parts.append(key_tok < limit)
        allowed.append(parts)
    stats = []
    todo = [(i, c) for i in range(len(sets)) for c in range(kv_heads)]

    def score(i, c):
        keys = [p[:, c * HEAD_DIM:(c + 1) * HEAD_DIM] for p in pieces]
        scores = lax.dot_general(
            jnp.concatenate(keys, axis=0) if len(keys) > 1 else keys[0], head_rows(query_refs[i], c),
            (((1,), (1,)), ((), ())), preferred_element_type=jnp.float32,
        )
        masked = [
            jnp.where(allowed[i][f], scores[f * FRAME_TOK:(f + 1) * FRAME_TOK], NEGATIVE) for f in range(len(tags))
        ]
        return jnp.concatenate(masked, axis=0) if len(masked) > 1 else masked[0]

    def weigh(i, c, scores):
        top = jnp.max(scores, axis=0, keepdims=True)
        shrink = None
        if not first:
            stat = states_in[2 * i + 1]
            old = stat[c:c + 1, :]
            top = jnp.maximum(top, old)
            shrink = jnp.exp2((old - top) * SCALE)
        weights = jnp.exp2((scores - top) * SCALE)
        total = jnp.sum(weights, axis=0, keepdims=True)
        if not first:
            total = total + stat[kv_heads + c:kv_heads + c + 1, :] * shrink
        return weights.astype(jnp.bfloat16), top, total, shrink

    def gather(i, c, weights, top, total, shrink):
        values = [p[:, (kv_heads + c) * HEAD_DIM:(kv_heads + c + 1) * HEAD_DIM] for p in pieces]
        weighted = lax.dot_general(
            jnp.concatenate(values, axis=0) if len(values) > 1 else values[0], weights,
            (((0,), (0,)), ((), ())), preferred_element_type=jnp.float32,
        )
        if not first:
            weighted = weighted + states_in[2 * i][c] * shrink
        if sent:
            states_out[0][c * HEAD_DIM:(c + 1) * HEAD_DIM, :] = weighted.astype(jnp.bfloat16)
            stats.append((top, total))
        else:
            states_out[2 * i][c] = weighted
            states_out[2 * i + 1][c:c + 1, :] = top
            states_out[2 * i + 1][kv_heads + c:kv_heads + c + 1, :] = total

    if len(todo) <= kv_heads:
        weighed = [weigh(*item, scores) for item, scores in [(item, score(*item)) for item in todo]]
        for item, done in zip(todo, weighed):
            gather(*item, *done)
    else:
        scores = score(*todo[0])
        before = None
        for n, item in enumerate(todo):
            following = score(*todo[n + 1]) if n + 1 < len(todo) else None
            done = weigh(*item, scores)
            if before is not None:
                gather(*todo[n - 1], *before)
            scores, before = following, done
        gather(*todo[-1], *before)
    if sent:
        rest = jnp.concatenate([top for top, _ in stats] + [total for _, total in stats], axis=0)
        parts = []
        for _ in range(3):
            parts.append(rest.astype(jnp.bfloat16).astype(jnp.float32))
            rest = rest - parts[-1]
        packed = jnp.concatenate(parts + [jnp.zeros_like(rest)], axis=0)
        states_out[0][kv_heads * HEAD_DIM:, :] = packed.astype(jnp.bfloat16)


def merge_kernel(acc_ref, stat_ref, got_ref, out_ref):
    kv_heads = acc_ref.shape[0]
    wide = kv_heads * HEAD_DIM
    parts = got_ref[wide:wide + 32, :].astype(jnp.float32)
    got_stat = parts[:8] + parts[8:16] + parts[16:24]
    for c in range(kv_heads):
        top, total = stat_ref[c:c + 1, :], stat_ref[kv_heads + c:kv_heads + c + 1, :]
        got_top, got_total = got_stat[c:c + 1, :], got_stat[kv_heads + c:kv_heads + c + 1, :]
        most = jnp.maximum(top, got_top)
        mine, theirs = jnp.exp2((top - most) * SCALE), jnp.exp2((got_top - most) * SCALE)
        share = 1.0 / (total * mine + got_total * theirs)
        result = acc_ref[c] * (mine * share) + got_ref[c * HEAD_DIM:(c + 1) * HEAD_DIM, :].astype(jnp.float32) * (theirs * share)
        result = result.astype(jnp.bfloat16)
        for r in range(GROUP):
            out_ref[:, (GROUP * c + r) * HEAD_DIM:(GROUP * c + r + 1) * HEAD_DIM] = (
                result[:, r * FRAME_TOK:(r + 1) * FRAME_TOK].T
            )


IN_SMEM = pl.BlockSpec(memory_space=pltpu.SMEM)
IN_VMEM = pl.BlockSpec(memory_space=pltpu.VMEM)
PARAMS = pltpu.CompilerParams(vmem_limit_bytes=20 * 1024 * 1024)


def attend(tags, sets, state, tables, queries, pieces, sent=False):
    kv_heads = kv_heads_of(pieces[0])
    rows = GROUP * FRAME_TOK
    out_shape = (
        jax.ShapeDtypeStruct((kv_heads, HEAD_DIM, rows), jnp.float32),
        jax.ShapeDtypeStruct((2 * kv_heads, rows), jnp.float32),
    ) * len(sets)
    if sent:
        out_shape = jax.ShapeDtypeStruct((kv_heads * HEAD_DIM + 32, rows), jnp.bfloat16)
    scores = rows * len(pieces) * FRAME_TOK * kv_heads * len(sets)
    return pl.pallas_call(
        functools.partial(attend_kernel, tags, sets, state is None, sent),
        out_shape=out_shape,
        in_specs=[IN_SMEM] * 3 + [IN_VMEM] * (len(sets) + len(pieces) + (0 if state is None else 2 * len(sets))),
        out_specs=IN_VMEM if sent else (IN_VMEM,) * (2 * len(sets)),
        compiler_params=PARAMS,
        cost_estimate=pl.CostEstimate(
            flops=4 * HEAD_DIM * scores, bytes_accessed=1024 * 1024, transcendentals=scores
        ),
    )(*tables, *queries, *pieces, *(() if state is None else state))


def merge(state, got, shape):
    return pl.pallas_call(
        merge_kernel,
        out_shape=jax.ShapeDtypeStruct(shape, jnp.bfloat16),
        in_specs=[IN_VMEM] * 3,
        out_specs=IN_VMEM,
        compiler_params=PARAMS,
        cost_estimate=pl.CostEstimate(flops=4 * shape[0] * shape[1], bytes_accessed=3 * 1024 * 1024, transcendentals=0),
    )(*state, got)


def on_device(queries, keys, values, frame_of, counts):
    blk = lax.axis_index("blk")
    where = jnp.stack([blk, lax.axis_index("head")]).astype(jnp.int32)
    starts_line = lax.rem(blk, NZ) == 0
    tables = (where, frame_of, counts)

    def either(first, other):
        return jnp.where(starts_line, first, other)

    own = jnp.concatenate([keys, values], axis=1)
    rows = own.shape[0]
    near1 = moved(own, next_group)
    cross0 = moved(own, other_column)
    in_near2 = inside(near1)
    both = (queries, moved(after(queries, near1), other_core))
    on_first = onward(jnp.concatenate([cross0, near1], axis=0))
    in_cross1 = inside(after(cross0, in_near2))
    on_second = onward(jnp.concatenate([in_cross1, in_near2], axis=0))
    cross1, near2 = either(on_first[:rows], in_cross1), either(on_first[rows:], in_near2)
    state = attend(((0, 0), (0, 1), (1, 0)), (0, 1), None, tables, both, (own, cross0, near1))
    in_cross2 = inside(after(cross1, state[1]))
    in_near3 = inside(near2)
    on_cross3 = onward(in_cross2)
    cross2 = either(on_second[:rows], in_cross2)
    in_cross3 = inside(cross2)
    near3 = either(after(on_second, cross2)[rows:], in_near3)
    state = attend(((2, 0), (1, 1), (3, 0), (2, 1)), (0, 1), state, tables, both, (near2, cross1, near3, cross2))
    cross3 = either(on_cross3, in_cross3)
    got = moved(attend(((3, 1),), (1,), state[2:], tables, both[1:], (cross3,), True), other_core)
    own_state = attend(((3, 1),), (0,), state[:2], tables, both[:1], (cross3,))
    return merge(own_state, got, queries.shape)


def solution(mesh):
    in_specs = (
        P(("blk", "head"), None),
        P(("blk", "head"), None),
        P(("blk", "head"), None),
        P(),
        P(),
    )
    out_specs = P(("blk", "head"), None)
    return jax.shard_map(
        on_device, mesh=mesh, in_specs=in_specs, out_specs=out_specs, check_vma=False
    )
```

```python
import functools
import math

import jax
import jax.numpy as jnp
from jax import lax
from jax.experimental import pallas as pl
from jax.experimental.pallas import tpu as pltpu
from jax.sharding import PartitionSpec as P

HEAD_DIM = 128
FRAME_TOK = 128
CYCLE = 4
NEGATIVE = -1e30
SCALE = math.log2(math.e) * HEAD_DIM ** (-0.5)

NX, NYLO, NYHI, NZ, NC = 4, 4, 2, 8, 2
AXES = ("blk", "head")
BLOCKS, GROUP_DEV = NX * NYLO * NZ, NYHI * NC
GROUP = 4


def flat(place):
    x, y, z, c = place
    return ((x * NYLO + y % NYLO) * NZ + z) * (NYHI * NC) + (y // NYLO) * NC + c


def places():
    for x in range(NX):
        for y in range(NYLO * NYHI):
            for z in range(NZ):
                for c in range(NC):
                    yield (x, y, z, c)


def next_group(place):
    x, y, z, c = place
    z += 1
    if z == NZ:
        z = 0
        if y % NYLO == NYLO - 1:
            x = (x + 1) % NX
        y = (y + 1) % (NYLO * NYHI)
    return (x, y, z, c)


def other_column(place):
    x, y, z, c = place
    return (x, (y + NYLO) % (NYLO * NYHI), z, c)


def other_core(place):
    x, y, z, c = place
    return (x, y, z, 1 - c)


def moved(value, target, sources=lambda place: True):
    return lax.ppermute(value, AXES, [(flat(p), flat(target(p))) for p in places() if sources(p)])


def inside(value):
    return moved(value, next_group, lambda place: place[2] != NZ - 1)


def onward(value):
    return moved(value, next_group, lambda place: place[2] == NZ - 1)


def after(value, *others):
    return lax.optimization_barrier((value, *others))[0]


def kv_heads_of(piece):
    return piece.shape[1] // (2 * HEAD_DIM)


def head_rows(query_ref, c):
    return jnp.concatenate(
        [query_ref[:, (GROUP * c + r) * HEAD_DIM:(GROUP * c + r + 1) * HEAD_DIM] for r in range(GROUP)], axis=0
    )


def piece_frame(blk, head, tag):
    offset, column = tag
    source = lax.rem(blk - offset + BLOCKS, BLOCKS)
    crossed = jnp.where(source // (NYLO * NZ) != blk // (NYLO * NZ), 1, 0)
    side = lax.rem(head // NC + crossed + column, NYHI)
    return source * GROUP_DEV + side * NC + lax.rem(head, NC)


def attend_kernel(tags, sets, first, sent, where_ref, frame_ref, count_ref, *refs):
    query_refs, refs = refs[: len(sets)], refs[len(sets):]
    pieces, refs = refs[: len(tags)], refs[len(tags):]
    if first:
        states_in, states_out = None, refs
    else:
        states_in, states_out = refs[: 2 * len(sets)], refs[2 * len(sets):]
    blk, head = where_ref[0], where_ref[1]
    kv_heads = kv_heads_of(pieces[0])
    rows = GROUP * FRAME_TOK
    key_tok = lax.broadcasted_iota(jnp.int32, (FRAME_TOK, rows), 0)
    query_tok = lax.rem(lax.broadcasted_iota(jnp.int32, (FRAME_TOK, rows), 1), FRAME_TOK)
    allowed = []
    for mate in sets:
        core = lax.rem(head + mate, NC)
        query_pos = frame_ref[blk * GROUP_DEV + head - lax.rem(head, NC) + core]
        parts = []
        for tag in tags:
            frame = piece_frame(blk, head, tag)
            if tag == (0, 0) and mate == 0:
                parts.append((key_tok <= query_tok) & (key_tok < count_ref[frame]))
            else:
                limit = jnp.where(frame_ref[frame] < query_pos, count_ref[frame], 0)
                parts.append(key_tok < limit)
        allowed.append(parts)
    stats = []
    todo = [(i, c) for i in range(len(sets)) for c in range(kv_heads)]

    def score(i, c):
        keys = [p[:, c * HEAD_DIM:(c + 1) * HEAD_DIM] for p in pieces]
        scores = lax.dot_general(
            jnp.concatenate(keys, axis=0) if len(keys) > 1 else keys[0], head_rows(query_refs[i], c),
            (((1,), (1,)), ((), ())), preferred_element_type=jnp.float32,
        )
        masked = [
            jnp.where(allowed[i][f], scores[f * FRAME_TOK:(f + 1) * FRAME_TOK], NEGATIVE) for f in range(len(tags))
        ]
        return jnp.concatenate(masked, axis=0) if len(masked) > 1 else masked[0]

    def weigh(i, c, scores):
        top = jnp.max(scores, axis=0, keepdims=True)
        shrink = None
        if not first:
            stat = states_in[2 * i + 1]
            old = stat[c:c + 1, :]
            top = jnp.maximum(top, old)
            shrink = jnp.exp2((old - top) * SCALE)
        weights = jnp.exp2((scores - top) * SCALE)
        total = jnp.sum(weights, axis=0, keepdims=True)
        if not first:
            total = total + stat[kv_heads + c:kv_heads + c + 1, :] * shrink
        return weights.astype(jnp.bfloat16), top, total, shrink

    def gather(i, c, weights, top, total, shrink):
        values = [p[:, (kv_heads + c) * HEAD_DIM:(kv_heads + c + 1) * HEAD_DIM] for p in pieces]
        weighted = lax.dot_general(
            jnp.concatenate(values, axis=0) if len(values) > 1 else values[0], weights,
            (((0,), (0,)), ((), ())), preferred_element_type=jnp.float32,
        )
        if not first:
            weighted = weighted + states_in[2 * i][c] * shrink
        if sent:
            states_out[0][c * HEAD_DIM:(c + 1) * HEAD_DIM, :] = weighted.astype(jnp.bfloat16)
            stats.append((top, total))
        else:
            states_out[2 * i][c] = weighted
            states_out[2 * i + 1][c:c + 1, :] = top
            states_out[2 * i + 1][kv_heads + c:kv_heads + c + 1, :] = total

    if len(todo) <= kv_heads:
        weighed = [weigh(*item, scores) for item, scores in [(item, score(*item)) for item in todo]]
        for item, done in zip(todo, weighed):
            gather(*item, *done)
    else:
        scores = score(*todo[0])
        before = None
        for n, item in enumerate(todo):
            following = score(*todo[n + 1]) if n + 1 < len(todo) else None
            done = weigh(*item, scores)
            if before is not None:
                gather(*todo[n - 1], *before)
            scores, before = following, done
        gather(*todo[-1], *before)
    if sent:
        rest = jnp.concatenate([top for top, _ in stats] + [total for _, total in stats], axis=0)
        parts = []
        for _ in range(3):
            parts.append(rest.astype(jnp.bfloat16).astype(jnp.float32))
            rest = rest - parts[-1]
        packed = jnp.concatenate(parts + [jnp.zeros_like(rest)], axis=0)
        states_out[0][kv_heads * HEAD_DIM:, :] = packed.astype(jnp.bfloat16)


def merge_kernel(acc_ref, stat_ref, got_ref, out_ref):
    kv_heads = acc_ref.shape[0]
    wide = kv_heads * HEAD_DIM
    parts = got_ref[wide:wide + 32, :].astype(jnp.float32)
    got_stat = parts[:8] + parts[8:16] + parts[16:24]
    for c in range(kv_heads):
        top, total = stat_ref[c:c + 1, :], stat_ref[kv_heads + c:kv_heads + c + 1, :]
        got_top, got_total = got_stat[c:c + 1, :], got_stat[kv_heads + c:kv_heads + c + 1, :]
        most = jnp.maximum(top, got_top)
        mine, theirs = jnp.exp2((top - most) * SCALE), jnp.exp2((got_top - most) * SCALE)
        share = 1.0 / (total * mine + got_total * theirs)
        result = acc_ref[c] * (mine * share) + got_ref[c * HEAD_DIM:(c + 1) * HEAD_DIM, :].astype(jnp.float32) * (theirs * share)
        result = result.astype(jnp.bfloat16)
        for r in range(GROUP):
            out_ref[:, (GROUP * c + r) * HEAD_DIM:(GROUP * c + r + 1) * HEAD_DIM] = (
                result[:, r * FRAME_TOK:(r + 1) * FRAME_TOK].T
            )


IN_SMEM = pl.BlockSpec(memory_space=pltpu.SMEM)
IN_VMEM = pl.BlockSpec(memory_space=pltpu.VMEM)
PARAMS = pltpu.CompilerParams(vmem_limit_bytes=20 * 1024 * 1024)


def attend(tags, sets, state, tables, queries, pieces, sent=False):
    kv_heads = kv_heads_of(pieces[0])
    rows = GROUP * FRAME_TOK
    out_shape = (
        jax.ShapeDtypeStruct((kv_heads, HEAD_DIM, rows), jnp.float32),
        jax.ShapeDtypeStruct((2 * kv_heads, rows), jnp.float32),
    ) * len(sets)
    if sent:
        out_shape = jax.ShapeDtypeStruct((kv_heads * HEAD_DIM + 32, rows), jnp.bfloat16)
    scores = rows * len(pieces) * FRAME_TOK * kv_heads * len(sets)
    return pl.pallas_call(
        functools.partial(attend_kernel, tags, sets, state is None, sent),
        out_shape=out_shape,
        in_specs=[IN_SMEM] * 3 + [IN_VMEM] * (len(sets) + len(pieces) + (0 if state is None else 2 * len(sets))),
        out_specs=IN_VMEM if sent else (IN_VMEM,) * (2 * len(sets)),
        compiler_params=PARAMS,
        cost_estimate=pl.CostEstimate(
            flops=4 * HEAD_DIM * scores, bytes_accessed=1024 * 1024, transcendentals=scores
        ),
    )(*tables, *queries, *pieces, *(() if state is None else state))


def merge(state, got, shape):
    return pl.pallas_call(
        merge_kernel,
        out_shape=jax.ShapeDtypeStruct(shape, jnp.bfloat16),
        in_specs=[IN_VMEM] * 3,
        out_specs=IN_VMEM,
        compiler_params=PARAMS,
        cost_estimate=pl.CostEstimate(flops=4 * shape[0] * shape[1], bytes_accessed=3 * 1024 * 1024, transcendentals=0),
    )(*state, got)


def on_device(queries, keys, values, frame_of, counts):
    blk = lax.axis_index("blk")
    where = jnp.stack([blk, lax.axis_index("head")]).astype(jnp.int32)
    starts_line = lax.rem(blk, NZ) == 0
    tables = (where, frame_of, counts)

    def either(first, other):
        return jnp.where(starts_line, first, other)

    own = jnp.concatenate([keys, values], axis=1)
    rows = own.shape[0]
    near1 = moved(own, next_group)
    cross0 = moved(own, other_column)
    in_near2 = inside(near1)
    both = (queries, moved(after(queries, near1), other_core))
    on_first = onward(jnp.concatenate([cross0, near1], axis=0))
    in_cross1 = inside(after(cross0, in_near2))
    on_second = onward(jnp.concatenate([in_cross1, in_near2], axis=0))
    cross1, near2 = either(on_first[:rows], in_cross1), either(on_first[rows:], in_near2)
    state = attend(((0, 0), (1, 0)), (0, 1), None, tables, both, (own, near1))
    in_cross2 = inside(after(cross1, state[1]))
    in_near3 = inside(near2)
    on_cross3 = onward(in_cross2)
    cross2 = either(on_second[:rows], in_cross2)
    in_cross3 = inside(cross2)
    near3 = either(after(on_second, cross2)[rows:], in_near3)
    state = attend(
        ((0, 1), (2, 0), (1, 1), (3, 0), (2, 1)), (0, 1), state, tables, both, (cross0, near2, cross1, near3, cross2)
    )
    cross3 = either(on_cross3, in_cross3)
    got = moved(attend(((3, 1),), (1,), state[2:], tables, both[1:], (cross3,), True), other_core)
    own_state = attend(((3, 1),), (0,), state[:2], tables, both[:1], (cross3,))
    return merge(own_state, got, queries.shape)


def solution(mesh):
    in_specs = (
        P(("blk", "head"), None),
        P(("blk", "head"), None),
        P(("blk", "head"), None),
        P(),
        P(),
    )
    out_specs = P(("blk", "head"), None)
    return jax.shard_map(
        on_device, mesh=mesh, in_specs=in_specs, out_specs=out_specs, check_vma=False
    )
```
